512 devices in a mesh: dp: 32 (over x, z), tensor: 16 (over y, core).
Axes of the slice: x: 4, y: 8, z: 8, core: 2. Of those that a mesh axis runs over, the one named last changes fastest.
Arguments:
- hidden: bfloat16 [8192, 18432], P('dp', 'tensor'), may hold values from -1.5 to 1.5
- grad_out: bfloat16 [8192, 2304], P('dp'), may hold values from -1.5 to 1.5
- q_init: bfloat16 [2304, 128], P('tensor'), may hold values from -6 to 6
- error: bfloat16 [32, 18432, 1152], P('dp', 'tensor'), may hold values from -6 to 6
Outputs:
- p_hat: bfloat16 [18432, 128], P('tensor')
- q_new: bfloat16 [2304, 128], P('tensor')
The draws below stay inside these ranges and needn't reach their ends.
All inputs are finite; a program needn't handle non-finite values.
Results may differ from the reference program's by a relative error of at most 0.0051.
Values may be sent and summed in bfloat16 or wider, within the bound.
No kernel may reach another device: no remote copies, remote signals or barrier semaphores. Data moves between devices by JAX's collectives and lax.ppermute only.
A program may use at most 64 MiB of HBM per device.

```python
import jax
import jax.numpy as jnp
from jax import lax

D = 2304
FF = 18432
RANK = 128
TOK_DEV = 256
REPLICAS = 16
TOKENS = 8192
N_DP = 32


def levels(key, shape, split, smallest, high):
    loudness, own = 1.0, jax.random.fold_in(key, 6)
    for position, parts in split:
        steps = jnp.exp(jax.random.uniform(jax.random.fold_in(own, position), (parts,), jnp.float32, smallest / len(split), high / len(split)))
        loudness = loudness * jnp.repeat(steps, shape[position] // parts).reshape([-1 if axis == position else 1 for axis in range(len(shape))])
    return loudness


def scatter_about(stream_key, dims, scale, most, cuts=(), dtype=jnp.bfloat16):
    result = jax.random.normal(stream_key, dims, jnp.float32) * scale
    if len(cuts) > 0:
        result = levels(stream_key, dims, cuts, -0.22, 0.18) * result
    return jnp.clip(result, min=-most, max=most).astype(dtype)


def setup_inputs(seed: int = 0) -> dict:
    key_of = jax.random.split(jax.random.key(seed), 5)
    hidden = scatter_about(key_of[0], (TOKENS, FF), 0.25, 1.5, ((0, 32), (1, 16)))
    grad_out = scatter_about(key_of[1], (TOKENS, D), 0.25, 1.5, ((0, 32),))
    q_init = scatter_about(key_of[2], (D, RANK), 1.0, 6.0, ((0, 16),))
    error = scatter_about(key_of[3], (N_DP, FF, D // 2), 1.0, 6.0, ((0, 32), (1, 16)))
    return {"hidden": hidden, "grad_out": grad_out, "q_init": q_init, "error": error}


def reference(hidden, grad_out, q_init, error):
    hid_blocks = hidden.reshape(REPLICAS, 2 * TOK_DEV, FF)
    out_blocks = grad_out.reshape(REPLICAS, 2 * TOK_DEV, D)
    err_blocks = error.reshape(REPLICAS, 2, FF, D // 2)

    def corrected_of(index):
        grad_w = lax.dot_general(hid_blocks[index].astype(jnp.float32), out_blocks[index].astype(jnp.float32), (((0,), (0,)), ((), ())), preferred_element_type=jnp.float32)
        pieces = err_blocks[index]
        joined = jnp.concatenate([pieces[0], pieces[1]], axis=1).astype(jnp.float32)
        return (grad_w + joined).astype(jnp.bfloat16)

    def p_step(total, index):
        return (total + jnp.dot(corrected_of(index).astype(jnp.float32), q_init.astype(jnp.float32), preferred_element_type=jnp.float32), None)
    p_total, _ = lax.scan(p_step, jnp.zeros((FF, RANK), jnp.float32), jnp.arange(REPLICAS))
    p_sum = p_total / REPLICAS
    gram = jnp.dot(p_sum.T, p_sum, precision=lax.Precision.HIGHEST)
    low = jnp.linalg.cholesky(gram)
    p_hat = lax.linalg.triangular_solve(low, p_sum, left_side=False, lower=True, transpose_a=True)
    p_round = p_hat.astype(jnp.bfloat16)

    def q_step(total, index):
        term = lax.dot_general(corrected_of(index).astype(jnp.float32), p_round.astype(jnp.float32), (((0,), (0,)), ((), ())), preferred_element_type=jnp.float32)
        return (total + term, None)
    q_total, _ = lax.scan(q_step, jnp.zeros((D, RANK), jnp.float32), jnp.arange(REPLICAS))
    return (p_round, (q_total / REPLICAS).astype(jnp.bfloat16))
```

```python
import jax
import jax.numpy as jnp
from jax import lax
from jax.sharding import PartitionSpec as P

F32 = jnp.float32
BF16 = jnp.bfloat16


def swap_blocks(blocks, axis):
    return lax.all_to_all(blocks, axis, 0, 0, tiled=True)


def spread(block, axis):
    return swap_blocks(jnp.broadcast_to(block, (lax.axis_size(axis),) + block.shape), axis)


def dot_rows(a, b):
    return lax.dot_general(a, b, (((0,), (0,)), ((), ())), preferred_element_type=F32)


def shards(hidden, grad_out, q_init, error):
    n_dp, n_tensor = lax.axis_size("dp"), lax.axis_size("tensor")
    replicas = n_dp // 2
    place = lax.axis_index("dp")
    side = place % 2
    width = grad_out.shape[1]
    half = width // 2
    rows, rank = hidden.shape[1], q_init.shape[1]
    err = error[0]

    q_whole = lax.all_gather(q_init, "tensor", axis=0, tiled=True)
    q_mine = lax.dynamic_slice_in_dim(q_whole, side * half, half, 0)
    mixed = jnp.dot(grad_out, q_whole, preferred_element_type=F32).astype(BF16)
    term = dot_rows(hidden, mixed) + jnp.dot(err, q_mine, preferred_element_type=F32)

    chunk = -(-rows // (n_dp * 8)) * 8
    padded = jnp.pad(term, ((0, chunk * n_dp - rows), (0, 0))).reshape(n_dp, chunk, rank)
    p_chunk = jnp.sum(swap_blocks(padded, "dp"), axis=0) / replicas
    p_sum = spread(p_chunk, "dp").reshape(n_dp * chunk, rank)[:rows]

    p_low = p_sum.astype(BF16)
    gram_part = jnp.dot(p_sum.T, p_sum, precision=lax.Precision.HIGHEST)
    hid_p = jnp.dot(hidden, p_low, preferred_element_type=F32).astype(BF16)
    from_err = dot_rows(err, p_low)
    s_part = dot_rows(grad_out, hid_p)
    zero = jnp.zeros_like(from_err)
    s_part = s_part + jnp.where(
        side == 0,
        jnp.concatenate([from_err, zero], axis=0),
        jnp.concatenate([zero, from_err], axis=0),
    )

    block = width // n_tensor
    gram_rows = rank // replicas
    gram_mine = lax.dynamic_slice_in_dim(gram_part, (place // 2) * gram_rows, gram_rows, 0)
    packet = jnp.concatenate(
        [
            s_part.reshape(n_tensor, block, rank),
            jnp.broadcast_to(gram_mine, (n_tensor, gram_rows, rank)),
        ],
        axis=1,
    )
    packet = jnp.sum(swap_blocks(packet, "tensor"), axis=0)
    packets = spread(packet, "dp")
    s_sum = jnp.sum(packets[:, :block], axis=0) / replicas
    gram = packets[::2, block:].reshape(rank, rank)

    low = jnp.linalg.cholesky(gram)
    both = lax.linalg.triangular_solve(
        low, jnp.concatenate([p_sum, s_sum], axis=0), left_side=False, lower=True, transpose_a=True
    )
    both = both.astype(BF16)
    return both[:rows], both[rows:]


def solution(mesh):
    in_specs = (P("dp", "tensor"), P("dp", None), P("tensor", None), P("dp", "tensor", None))
    out_specs = (P("tensor", None), P("tensor", None))
    return jax.shard_map(shards, mesh=mesh, in_specs=in_specs, out_specs=out_specs, check_vma=False)
```

```python
import functools

import jax
import jax.numpy as jnp
from jax import lax
from jax.experimental import pallas as pl
from jax.experimental.pallas import tpu as pltpu
from jax.sharding import Mesh
from jax.sharding import PartitionSpec as P

F32 = jnp.float32
BF16 = jnp.bfloat16
DP = ("x", "z")
TENSOR = ("y", "core")
VMEM_BYTES = 32 * 2**20
STEP = 8


def swap_blocks(blocks, axis):
    return lax.all_to_all(blocks, axis, 0, 0, tiled=True)


def dot(a, b):
    return jnp.dot(a, b, preferred_element_type=F32)


def dot_rows(a, b):
    return lax.dot_general(a, b, (((0,), (0,)), ((), ())), preferred_element_type=F32)


def dot_cols(a, b):
    return lax.dot_general(a, b, (((1,), (1,)), ((), ())), preferred_element_type=F32)


def round_up(count, multiple):
    return -(-count // multiple) * multiple


def two_terms(value):
    high = value.astype(BF16)
    rest = (value - high.astype(F32)).astype(BF16)
    return high, rest


def three_terms(value):
    high = value.astype(BF16)
    rest = value - high.astype(F32)
    middle = rest.astype(BF16)
    low = (rest - middle.astype(F32)).astype(BF16)
    return high.astype(F32), middle.astype(F32), low.astype(F32)


def call(kernel, out_shapes, scratch, flops, bytes_accessed, in_specs):
    return pl.pallas_call(
        kernel,
        out_shape=out_shapes,
        in_specs=in_specs,
        scratch_shapes=scratch,
        compiler_params=pltpu.CompilerParams(vmem_limit_bytes=VMEM_BYTES),
        cost_estimate=pl.CostEstimate(flops=flops, bytes_accessed=bytes_accessed, transcendentals=0),
    )


IN_VMEM = pl.BlockSpec(memory_space=pltpu.VMEM)
IN_SMEM = pl.BlockSpec(memory_space=pltpu.SMEM)
ANYWHERE = pl.BlockSpec(memory_space=pl.ANY)


def fetch(sources, targets, sems):
    copies = []
    for index, (source, target) in enumerate(zip(sources, targets)):
        copies.append(pltpu.make_async_copy(source, target, sems.at[index]))
        copies[-1].start()
    return copies


def left_term_kernel(cuts, place_ref, hid_hbm, out_hbm, err_hbm, q_ref, o_ref, hid, out, err, sems):
    rows = hid.shape[1]
    half = err.shape[1]
    slab = rows // cuts
    sources = [out_hbm, hid_hbm] + [err_hbm.at[0, pl.ds(i * slab, slab)] for i in range(cuts)]
    targets = [out, hid] + [err.at[pl.ds(i * slab, slab)] for i in range(cuts)]
    copies = fetch(sources, targets, sems)
    copies[0].wait()
    high, rest = two_terms(dot(out[...], q_ref[...]))
    both = jnp.concatenate([high, rest], axis=1)
    copies[1].wait()
    turned = dot_rows(both, hid[...])
    rank = high.shape[1]
    turned = jnp.transpose(turned[:rank] + turned[rank:])
    side = place_ref[1] % 2
    q_mine = q_ref[pl.ds(pl.multiple_of(side * half, 128), half), :]
    terms = []
    for i in range(cuts):
        copies[2 + i].wait()
        part = dot(err[pl.ds(i * slab, slab), :], q_mine)
        terms.append(part + turned[i * slab : (i + 1) * slab])
    term = jnp.concatenate(terms, axis=0)
    blocks, chunk, _ = o_ref.shape
    for i in range(blocks):
        piece = term[min(i * chunk, rows) : min((i + 1) * chunk, rows)]
        missing = chunk - piece.shape[0]
        if missing == chunk:
            piece = jnp.zeros((chunk, rank), F32)
        elif missing:
            piece = jnp.concatenate([piece, jnp.zeros((missing, rank), F32)], axis=0)
        o_ref[i] = piece.astype(BF16)


def left_term(place, hidden, grad_out, error, q_whole, blocks, chunk):
    tokens, rows = hidden.shape
    width, rank = q_whole.shape
    half = error.shape[2]
    cuts = 4
    return call(
        functools.partial(left_term_kernel, cuts),
        jax.ShapeDtypeStruct((blocks, chunk, rank), BF16),
        [
            pltpu.VMEM((tokens, rows), BF16),
            pltpu.VMEM((tokens, width), BF16),
            pltpu.VMEM((rows, half), BF16),
            pltpu.SemaphoreType.DMA((2 + cuts,)),
        ],
        2 * rank * (tokens * (width + rows) + rows * half),
        2 * (tokens * (width + rows) + rows * half + width * rank),
        [IN_SMEM, ANYWHERE, ANYWHERE, ANYWHERE, IN_VMEM],
    )(place, hidden, grad_out, error, q_whole)


def mean_kernel(scale, in_ref, o_ref):
    blocks = in_ref.shape[0]
    total = in_ref[0].astype(F32)
    for i in range(1, blocks):
        total += in_ref[i].astype(F32)
    total = (total * scale).astype(BF16)
    for i in range(blocks):
        o_ref[i] = total


def mean_of_blocks(blocks, scale):
    return call(
        functools.partial(mean_kernel, scale),
        jax.ShapeDtypeStruct(blocks.shape, BF16),
        [],
        blocks.size,
        4 * blocks.size,
        [IN_VMEM],
    )(blocks)


def packet_kernel(n_x, n_z, cuts, place_ref, hid_hbm, out_hbm, err_hbm, p_ref, o_ref, hid, out, err, turned, flat, pack, gram, sems):
    tokens, rows = hid.shape
    width = out.shape[1]
    half = err.shape[1]
    rank = p_ref.shape[1]
    slab = rows // cuts
    sources = [hid_hbm] + [err_hbm.at[0, pl.ds(i * slab, slab)] for i in range(cuts)] + [out_hbm]
    targets = [hid] + [err.at[pl.ds(i * slab, slab)] for i in range(cuts)] + [out]
    copies = fetch(sources, targets, sems)
    x, z = place_ref[0], place_ref[1]
    quarter = rows // n_x
    p_quarter = p_ref[pl.ds(pl.multiple_of(x * quarter, 16), quarter), :]
    gram[...] = dot_rows(p_quarter, p_quarter)
    copies[0].wait()
    high, rest = two_terms(dot(hid[...], p_ref[:rows, :]))
    both = jnp.concatenate([high, rest], axis=1)
    from_err = jnp.zeros((rank, half), F32)
    for i in range(cuts):
        copies[1 + i].wait()
        from_err += dot_rows(p_ref[i * slab : (i + 1) * slab, :], err[pl.ds(i * slab, slab), :])
    copies[1 + cuts].wait()
    from_out = dot_rows(both, out[...])
    turned[...] = from_out[:rank] + from_out[rank:]
    side = z % 2
    mine = pl.ds(pl.multiple_of(side * half, 128), half)
    turned[:, mine] += from_err
    for i in range(width // rank):
        flat[i * rank : (i + 1) * rank, :] = jnp.transpose(turned[:, i * rank : (i + 1) * rank])
    count = o_ref.shape[0]
    piece = width // count
    few = rank // (n_x * n_z)
    own = gram[pl.ds(pl.multiple_of(z * (few * n_x), 8), few * n_x), :]
    terms = three_terms(own)
    for i in range(count):
        at = i % n_x
        pack[i, 0:piece, :] = flat[i * piece : (i + 1) * piece, :]
        for j, term in enumerate(terms):
            pack[i, piece + j * few : piece + (j + 1) * few, :] = term[at * few : (at + 1) * few]
    o_ref[...] = pack[...].astype(BF16)


def packets_of(place, hidden, grad_out, error, p_sum, n_x, n_z, n_tensor):
    tokens, rows = hidden.shape
    width = grad_out.shape[1]
    half = error.shape[2]
    rank = p_sum.shape[1]
    cuts = 4
    count = n_tensor * n_x
    deep = width // count + 3 * (rank // (n_x * n_z))
    return call(
        functools.partial(packet_kernel, n_x, n_z, cuts),
        jax.ShapeDtypeStruct((count, deep, rank), BF16),
        [
            pltpu.VMEM((tokens, rows), BF16),
            pltpu.VMEM((tokens, width), BF16),
            pltpu.VMEM((rows, half), BF16),
            pltpu.VMEM((rank, width), F32),
            pltpu.VMEM((width, rank), F32),
            pltpu.VMEM((count, deep, rank), F32),
            pltpu.VMEM((rank, rank), F32),
            pltpu.SemaphoreType.DMA((2 + cuts,)),
        ],
        2 * rank * (tokens * (width + rows) + rows * half),
        2 * (tokens * (width + rows) + rows * half + rows * rank),
        [IN_SMEM, ANYWHERE, ANYWHERE, ANYWHERE, IN_VMEM],
    )(place, hidden, grad_out, error, p_sum)


def repack_kernel(few, in_ref, o_ref, pack):
    count, deep, rank = in_ref.shape
    piece = deep - 3 * few
    total = in_ref[0].astype(F32)
    for i in range(1, count):
        total += in_ref[i].astype(F32)
    pack[...] = total
    rows = [pack[piece + j * few : piece + (j + 1) * few, :] for j in range(3)]
    for j, term in enumerate(three_terms((rows[2] + rows[1]) + rows[0])):
        pack[piece + j * few : piece + (j + 1) * few, :] = term
    packet = pack[...].astype(BF16)
    for i in range(o_ref.shape[0]):
        o_ref[i] = packet


def repacked(packets, few, n_dp):
    count, deep, rank = packets.shape
    return call(
        functools.partial(repack_kernel, few),
        jax.ShapeDtypeStruct((n_dp, deep, rank), BF16),
        [pltpu.VMEM((deep, rank), F32)],
        packets.size,
        4 * packets.size,
        [IN_VMEM],
    )(packets)


def small_factor(block, like):
    size = block.shape[0]
    a = {}
    for i in range(size):
        for j in range(i + 1):
            a[i, j] = jnp.broadcast_to(block[i : i + 1, j : j + 1], like)
    inverse = {}
    for j in range(size):
        pivot = a[j, j]
        scale = lax.rsqrt(pivot)
        scale = scale * (1.5 - (0.5 * pivot) * (scale * scale))
        for m in range(j):
            inverse[j, m] = inverse[j, m] * scale
        inverse[j, j] = scale
        column = {i: a[i, j] * scale for i in range(j + 1, size)}
        for i in range(j + 1, size):
            for m in range(j + 1, i + 1):
                a[i, m] = a[i, m] - column[i] * column[m]
            for m in range(j + 1):
                step = column[i] * inverse[j, m]
                inverse[i, m] = inverse[i, m] - step if (i, m) in inverse else -step
    return inverse


def inverse_factor(gram):
    rank = gram.shape[0]
    like = (STEP, rank)
    lane = lax.broadcasted_iota(jnp.int32, like, 1)
    tiles = [gram[b * STEP : (b + 1) * STEP, :] for b in range(rank // STEP)]
    done = []
    for k in range(rank // STEP):
        first = k * STEP
        inverse = small_factor(tiles[k][:, first : first + STEP], like)
        inside = (lane >= first) & (lane < first + STEP)
        pivots = []
        for m in range(STEP):
            row = jnp.broadcast_to(tiles[k][m : m + 1, :], like)
            pivots.append(jnp.where(inside, jnp.where(lane == first + m, 1.0, 0.0), row))
        scaled = []
        for i in range(STEP):
            row = inverse[i, 0] * pivots[0]
            for m in range(1, i + 1):
                row = row + inverse[i, m] * pivots[m]
            scaled.append(row)
        sublane = lax.broadcasted_iota(jnp.int32, like, 0)
        rows = scaled[0]
        for i in range(1, STEP):
            rows = jnp.where(sublane == i, scaled[i], rows)
        done.append(jnp.where(lane <= first + sublane, rows, 0.0))
        for b in range(k + 1, rank // STEP):
            columns = [
                jnp.broadcast_to(tiles[b][:, first + m : first + m + 1], like) for m in range(STEP)
            ]
            tile = jnp.where(inside, 0.0, tiles[b])
            for i in range(STEP):
                factor = inverse[i, 0] * columns[0]
                for m in range(1, i + 1):
                    factor = factor + inverse[i, m] * columns[m]
                tile = tile - factor * scaled[i]
            tiles[b] = tile
    return jnp.concatenate(done, axis=0)


def finish_kernel(scale, pick_ref, in_ref, p_ref, p_out, q_out):
    rank = p_ref.shape[1]
    summed = dot(pick_ref[...], in_ref[...])
    inverse = inverse_factor(summed[:rank])
    s_sum = summed[rank:] * scale
    terms = [term.astype(BF16) for term in three_terms(inverse)]
    p_low = p_ref[: p_out.shape[0], :]
    p_new = dot_cols(p_low, terms[2]) + dot_cols(p_low, terms[1])
    p_out[...] = (p_new + dot_cols(p_low, terms[0])).astype(BF16)
    q_new = lax.dot_general(
        s_sum,
        inverse,
        (((1,), (1,)), ((), ())),
        precision=lax.Precision.HIGHEST,
        preferred_element_type=F32,
    )
    q_out[...] = q_new.astype(BF16)


def pick_rows(n_x, n_z, piece, few, rank):
    deep = piece + 3 * few
    count = n_x * n_z
    source = lax.broadcasted_iota(jnp.int32, (1, count * deep), 1)
    device, row = source // deep, source % deep
    x, z = device // n_z, device % n_z
    gram_row = z * (few * n_x) + x * few + (row - piece) % few
    factor_row = rank + x * piece + row
    target = jnp.where(row < piece, factor_row, gram_row)
    rows = lax.broadcasted_iota(jnp.int32, (rank + n_x * piece, 1), 0)
    return (rows == target).astype(BF16)


def finished(packets, p_sum, rows, n_x, n_z, few):
    count, deep, rank = packets.shape
    piece = deep - 3 * few
    pick = pick_rows(n_x, n_z, piece, few, rank)
    return call(
        functools.partial(finish_kernel, 2.0 / count),
        (
            jax.ShapeDtypeStruct((rows, rank), BF16),
            jax.ShapeDtypeStruct((n_x * piece, rank), BF16),
        ),
        [],
        2 * rank * (pick.size + 3 * rows * rank),
        2 * (pick.size + 2 * rows * rank),
        [IN_VMEM, IN_VMEM, IN_VMEM],
    )(pick, packets.reshape(count * deep, rank), p_sum)


def shards(hidden, grad_out, q_init, error):
    n_x, n_z = lax.axis_size("x"), lax.axis_size("z")
    n_dp, n_tensor = lax.axis_size(DP), lax.axis_size(TENSOR)
    replicas = n_dp // 2
    place = jnp.stack([lax.axis_index("x"), lax.axis_index("z")]).astype(jnp.int32)
    rows, rank = hidden.shape[1], q_init.shape[1]
    few = rank // n_dp
    chunk = round_up(-(-rows // n_dp), 8)

    q_whole = lax.all_gather(q_init, TENSOR, axis=0, tiled=True)
    pieces = left_term(place, hidden, grad_out, error, q_whole, n_dp, chunk)
    pieces = mean_of_blocks(swap_blocks(pieces, DP), 1.0 / replicas)
    p_sum = swap_blocks(pieces, DP).reshape(n_dp * chunk, rank)
    packets = packets_of(place, hidden, grad_out, error, p_sum, n_x, n_z, n_tensor)
    packets = repacked(swap_blocks(packets, TENSOR + ("x",)), few, n_dp)
    return finished(swap_blocks(packets, DP), p_sum, rows, n_x, n_z, few)


def solution(mesh):
    fine = Mesh(mesh.devices.reshape(4, 8, 8, 2), DP + TENSOR)
    in_specs = (P(DP, TENSOR), P(DP, None), P(TENSOR, None), P(DP, TENSOR, None))
    out_specs = (P(TENSOR, None), P(TENSOR, None))
    return jax.shard_map(shards, mesh=fine, in_specs=in_specs, out_specs=out_specs, check_vma=False)
```

```python
import functools

import jax
import jax.numpy as jnp
from jax import lax
from jax.experimental import pallas as pl
from jax.experimental.pallas import tpu as pltpu
from jax.sharding import Mesh
from jax.sharding import PartitionSpec as P

F32 = jnp.float32
BF16 = jnp.bfloat16
DP = ("x", "z")
TENSOR = ("y", "core")
VMEM_BYTES = 32 * 2**20
VMEM_MOST = 53 * 2**20
STEP = 8


def swap_blocks(blocks, axis):
    return lax.all_to_all(blocks, axis, 0, 0, tiled=True)


def dot(a, b):
    return jnp.dot(a, b, preferred_element_type=F32)


def dot_rows(a, b):
    return lax.dot_general(a, b, (((0,), (0,)), ((), ())), preferred_element_type=F32)


def dot_cols(a, b):
    return lax.dot_general(a, b, (((1,), (1,)), ((), ())), preferred_element_type=F32)


def round_up(count, multiple):
    return -(-count // multiple) * multiple


def two_terms(value):
    high = value.astype(BF16)
    rest = (value - high.astype(F32)).astype(BF16)
    return high, rest


def three_terms(value):
    high = value.astype(BF16)
    rest = value - high.astype(F32)
    middle = rest.astype(BF16)
    low = (rest - middle.astype(F32)).astype(BF16)
    return high.astype(F32), middle.astype(F32), low.astype(F32)


def call(kernel, out_shapes, scratch, flops, bytes_accessed, in_specs, vmem=VMEM_BYTES):
    return pl.pallas_call(
        kernel,
        out_shape=out_shapes,
        in_specs=in_specs,
        scratch_shapes=scratch,
        compiler_params=pltpu.CompilerParams(vmem_limit_bytes=vmem),
        cost_estimate=pl.CostEstimate(flops=flops, bytes_accessed=bytes_accessed, transcendentals=0),
    )


IN_VMEM = pl.BlockSpec(memory_space=pltpu.VMEM)
ANYWHERE = pl.BlockSpec(memory_space=pl.ANY)


def fetch(sources, targets, sems):
    copies = []
    for index, (source, target) in enumerate(zip(sources, targets)):
        copies.append(pltpu.make_async_copy(source, target, sems.at[index]))
        copies[-1].start()
    return copies


def token_term_kernel(hid_hbm, out_hbm, q_hbm, o_ref, own_ref, hid, out, q, sems):
    rank = q.shape[1]
    half = own_ref.shape[0]
    copies = fetch([q_hbm, out_hbm, hid_hbm], [q, out, hid], sems)
    side = lax.axis_index("z") % 2
    copies[0].wait()
    own_ref[...] = q[pl.ds(pl.multiple_of(side * half, 128), half), :]
    copies[1].wait()
    high, rest = two_terms(dot(out[...], q[...]))
    both = jnp.concatenate([high, rest], axis=1)
    copies[2].wait()
    turned = dot_rows(hid[...], both)
    o_ref[...] = turned[:, :rank] + turned[:, rank:]


def token_term(hidden, grad_out, q_whole, half):
    tokens, rows = hidden.shape
    width, rank = q_whole.shape
    return call(
        token_term_kernel,
        (
            jax.ShapeDtypeStruct((rows, rank), F32),
            jax.ShapeDtypeStruct((half, rank), BF16),
        ),
        [
            pltpu.VMEM((tokens, rows), BF16),
            pltpu.VMEM((tokens, width), BF16),
            pltpu.VMEM((width, rank), BF16),
            pltpu.SemaphoreType.DMA((3,)),
        ],
        2 * rank * tokens * (width + 2 * rows),
        2 * (tokens * (width + rows) + width * rank),
        [ANYWHERE] * 3,
        VMEM_MOST,
    )(hidden, grad_out, q_whole)


def left_term_kernel(err_ref, own_ref, token_ref, o_ref):
    rows, rank = token_ref.shape
    term = dot(err_ref[0], own_ref[...]) + token_ref[...]
    blocks, chunk, _ = o_ref.shape
    for i in range(blocks):
        piece = term[min(i * chunk, rows) : min((i + 1) * chunk, rows)]
        missing = chunk - piece.shape[0]
        if missing == chunk:
            piece = jnp.zeros((chunk, rank), F32)
        elif missing:
            piece = jnp.concatenate([piece, jnp.zeros((missing, rank), F32)], axis=0)
        o_ref[i] = piece.astype(BF16)


def left_term(error, q_own, tokens, blocks, chunk):
    rows, rank = tokens.shape
    half = error.shape[2]
    return call(
        left_term_kernel,
        jax.ShapeDtypeStruct((blocks, chunk, rank), BF16),
        [],
        2 * rank * rows * half,
        2 * (rows * half + half * rank),
        [IN_VMEM] * 3,
    )(error, q_own, tokens)


def mean_kernel(scale, in_ref, o_ref):
    blocks = in_ref.shape[0]
    total = in_ref[0].astype(F32)
    for i in range(1, blocks):
        total += in_ref[i].astype(F32)
    total = (total * scale).astype(BF16)
    for i in range(blocks):
        o_ref[i] = total


def mean_of_blocks(blocks, scale):
    return call(
        functools.partial(mean_kernel, scale),
        jax.ShapeDtypeStruct(blocks.shape, BF16),
        [],
        blocks.size,
        4 * blocks.size,
        [IN_VMEM],
    )(blocks)


def right_term_kernel(n_x, n_tensor, hid_ref, out_ref, err_ref, p_ref, send_ref, keep_ref, turned, flat, gram):
    rows = hid_ref.shape[1]
    width = out_ref.shape[1]
    half = err_ref.shape[2]
    rank = p_ref.shape[1]
    x, z, core = (lax.axis_index(axis) for axis in ("x", "z", "core"))
    quarter = rows // n_x
    p_quarter = p_ref[pl.ds(pl.multiple_of(x * quarter, 16), quarter), :]
    gram[...] = dot_rows(p_quarter, p_quarter)
    p_own = p_ref[:rows, :]
    high, rest = two_terms(dot(hid_ref[...], p_own))
    both = jnp.concatenate([high, rest], axis=1)
    from_err = dot_rows(p_own, err_ref[0])
    from_out = dot_rows(both, out_ref[...])
    turned[...] = from_out[:rank] + from_out[rank:]
    side = z % 2
    mine = pl.ds(pl.multiple_of(side * half, 128), half)
    turned[:, mine] += from_err
    for i in range(width // rank):
        flat[i * rank : (i + 1) * rank, :] = jnp.transpose(turned[:, i * rank : (i + 1) * rank])
    block = width // n_tensor
    blocks = n_tensor // 2
    for target, owner in ((send_ref, 1 - core), (keep_ref, core)):
        for i in range(blocks):
            start = pl.multiple_of((2 * i + owner) * block, 8)
            target[i * block : (i + 1) * block, :] = flat[pl.ds(start, block), :]
        few = target.shape[0] - blocks * block
        target[blocks * block :, :] = gram[pl.ds(pl.multiple_of(z * few, 8), few), :]


def right_terms(hidden, grad_out, error, p_sum, n_x, n_z, n_tensor):
    tokens, rows = hidden.shape
    width = grad_out.shape[1]
    half = error.shape[2]
    rank = p_sum.shape[1]
    kept = jax.ShapeDtypeStruct((width // 2 + rank // n_z, rank), F32)
    return call(
        functools.partial(right_term_kernel, n_x, n_tensor),
        (kept, kept),
        [
            pltpu.VMEM((rank, width), F32),
            pltpu.VMEM((width, rank), F32),
            pltpu.VMEM((rank, rank), F32),
        ],
        2 * rank * (tokens * (width + rows) + rows * half),
        2 * (tokens * (width + rows) + rows * half + rows * rank),
        [IN_VMEM] * 4,
    )(hidden, grad_out, error, p_sum)


def pack_kernel(n_x, piece, few, keep_ref, came_ref, o_ref, total, pack):
    total[...] = keep_ref[...] + came_ref[...]
    count = o_ref.shape[0]
    terms = three_terms(total[count * piece :, :])
    for i in range(count):
        at = i % n_x
        pack[i, 0:piece, :] = total[i * piece : (i + 1) * piece, :]
        for j, term in enumerate(terms):
            pack[i, piece + j * few : piece + (j + 1) * few, :] = term[at * few : (at + 1) * few]
    o_ref[...] = pack[...].astype(BF16)


def packets_of(kept, came, n_x, count, few):
    rows, rank = kept.shape
    piece = (rows - n_x * few) // count
    deep = piece + 3 * few
    return call(
        functools.partial(pack_kernel, n_x, piece, few),
        jax.ShapeDtypeStruct((count, deep, rank), BF16),
        [pltpu.VMEM((rows, rank), F32), pltpu.VMEM((count, deep, rank), F32)],
        rows * rank,
        8 * rows * rank + 2 * count * deep * rank,
        [IN_VMEM, IN_VMEM],
    )(kept, came)


def repack_kernel(few, in_ref, o_ref, pack):
    count, deep, rank = in_ref.shape
    piece = deep - 3 * few
    total = in_ref[0].astype(F32)
    for i in range(1, count):
        total += in_ref[i].astype(F32)
    pack[...] = total
    rows = [pack[piece + j * few : piece + (j + 1) * few, :] for j in range(3)]
    for j, term in enumerate(three_terms((rows[2] + rows[1]) + rows[0])):
        pack[piece + j * few : piece + (j + 1) * few, :] = term
    packet = pack[...].astype(BF16)
    for i in range(o_ref.shape[0]):
        o_ref[i] = packet


def repacked(packets, few, n_dp):
    count, deep, rank = packets.shape
    return call(
        functools.partial(repack_kernel, few),
        jax.ShapeDtypeStruct((n_dp, deep, rank), BF16),
        [pltpu.VMEM((deep, rank), F32)],
        packets.size,
        4 * packets.size,
        [IN_VMEM],
    )(packets)


def small_factor(block, like):
    size = block.shape[0]
    a = {}
    for i in range(size):
        for j in range(i + 1):
            a[i, j] = jnp.broadcast_to(block[i : i + 1, j : j + 1], like)
    inverse = {}
    for j in range(size):
        pivot = a[j, j]
        scale = lax.rsqrt(pivot)
        scale = scale * (1.5 - (0.5 * pivot) * (scale * scale))
        for m in range(j):
            inverse[j, m] = inverse[j, m] * scale
        inverse[j, j] = scale
        column = {i: a[i, j] * scale for i in range(j + 1, size)}
        for i in range(j + 1, size):
            for m in range(j + 1, i + 1):
                a[i, m] = a[i, m] - column[i] * column[m]
            for m in range(j + 1):
                step = column[i] * inverse[j, m]
                inverse[i, m] = inverse[i, m] - step if (i, m) in inverse else -step
    return inverse


def inverse_factor(gram):
    rank = gram.shape[0]
    like = (STEP, rank)
    lane = lax.broadcasted_iota(jnp.int32, like, 1)
    tiles = [gram[b * STEP : (b + 1) * STEP, :] for b in range(rank // STEP)]
    done = []
    for k in range(rank // STEP):
        first = k * STEP
        inverse = small_factor(tiles[k][:, first : first + STEP], like)
        inside = (lane >= first) & (lane < first + STEP)
        pivots = []
        for m in range(STEP):
            row = jnp.broadcast_to(tiles[k][m : m + 1, :], like)
            pivots.append(jnp.where(inside, jnp.where(lane == first + m, 1.0, 0.0), row))
        scaled = []
        for i in range(STEP):
            row = inverse[i, 0] * pivots[0]
            for m in range(1, i + 1):
                row = row + inverse[i, m] * pivots[m]
            scaled.append(row)
        sublane = lax.broadcasted_iota(jnp.int32, like, 0)
        rows = scaled[0]
        for i in range(1, STEP):
            rows = jnp.where(sublane == i, scaled[i], rows)
        done.append(jnp.where(lane <= first + sublane, rows, 0.0))
        for b in range(k + 1, rank // STEP):
            columns = [
                jnp.broadcast_to(tiles[b][:, first + m : first + m + 1], like) for m in range(STEP)
            ]
            tile = jnp.where(inside, 0.0, tiles[b])
            for i in range(STEP):
                factor = inverse[i, 0] * columns[0]
                for m in range(1, i + 1):
                    factor = factor + inverse[i, m] * columns[m]
                tile = tile - factor * scaled[i]
            tiles[b] = tile
    return jnp.concatenate(done, axis=0)


def finish_kernel(scale, pick_ref, in_ref, p_ref, p_out, q_out):
    rank = p_ref.shape[1]
    summed = dot(pick_ref[...], in_ref[...])
    inverse = inverse_factor(summed[:rank])
    s_sum = summed[rank:] * scale
    terms = [term.astype(BF16) for term in three_terms(inverse)]
    p_low = p_ref[: p_out.shape[0], :]
    p_new = dot_cols(p_low, terms[2]) + dot_cols(p_low, terms[1])
    p_out[...] = (p_new + dot_cols(p_low, terms[0])).astype(BF16)
    q_new = lax.dot_general(
        s_sum,
        inverse,
        (((1,), (1,)), ((), ())),
        precision=lax.Precision.HIGHEST,
        preferred_element_type=F32,
    )
    q_out[...] = q_new.astype(BF16)


def pick_rows(n_x, n_z, piece, few, rank):
    deep = piece + 3 * few
    count = n_x * n_z
    source = lax.broadcasted_iota(jnp.int32, (1, count * deep), 1)
    device, row = source // deep, source % deep
    x, z = device // n_z, device % n_z
    gram_row = z * (few * n_x) + x * few + (row - piece) % few
    factor_row = rank + x * piece + row
    target = jnp.where(row < piece, factor_row, gram_row)
    rows = lax.broadcasted_iota(jnp.int32, (rank + n_x * piece, 1), 0)
    return (rows == target).astype(BF16)


def finished(packets, p_sum, rows, n_x, n_z, few):
    count, deep, rank = packets.shape
    piece = deep - 3 * few
    pick = pick_rows(n_x, n_z, piece, few, rank)
    return call(
        functools.partial(finish_kernel, 2.0 / count),
        (
            jax.ShapeDtypeStruct((rows, rank), BF16),
            jax.ShapeDtypeStruct((n_x * piece, rank), BF16),
        ),
        [],
        2 * rank * (pick.size + 3 * rows * rank),
        2 * (pick.size + 2 * rows * rank),
        [IN_VMEM, IN_VMEM, IN_VMEM],
    )(pick, packets.reshape(count * deep, rank), p_sum)


def shards(hidden, grad_out, q_init, error):
    n_x, n_z = lax.axis_size("x"), lax.axis_size("z")
    n_dp, n_tensor = lax.axis_size(DP), lax.axis_size(TENSOR)
    replicas = n_dp // 2
    rows, rank = hidden.shape[1], q_init.shape[1]
    few = rank // n_dp
    chunk = round_up(-(-rows // n_dp), 8)

    q_whole = lax.all_gather(q_init, TENSOR, axis=0, tiled=True)
    tokens, q_own = token_term(hidden, grad_out, q_whole, error.shape[2])
    pieces = left_term(error, q_own, tokens, n_dp, chunk)
    pieces = mean_of_blocks(swap_blocks(pieces, DP), 1.0 / replicas)
    p_sum = swap_blocks(pieces, DP).reshape(n_dp * chunk, rank)
    sent, kept = right_terms(hidden, grad_out, error, p_sum, n_x, n_z, n_tensor)
    came = lax.ppermute(sent, "core", [(0, 1), (1, 0)])
    packets = packets_of(kept, came, n_x, n_x * (n_tensor // 2), few)
    packets = repacked(swap_blocks(packets, ("y", "x")), few, n_dp)
    return finished(swap_blocks(packets, DP), p_sum, rows, n_x, n_z, few)


def solution(mesh):
    fine = Mesh(mesh.devices.reshape(4, 8, 8, 2), DP + TENSOR)
    in_specs = (P(DP, TENSOR), P(DP, None), P(TENSOR, None), P(DP, TENSOR, None))
    out_specs = (P(TENSOR, None), P(TENSOR, None))
    return jax.shard_map(shards, mesh=fine, in_specs=in_specs, out_specs=out_specs, check_vma=False)
```

```python
import functools

import jax
import jax.numpy as jnp
import ml_dtypes
import numpy as np
from jax import lax
from jax.experimental import pallas as pl
from jax.experimental.pallas import tpu as pltpu
from jax.sharding import Mesh
from jax.sharding import PartitionSpec as P

F32 = jnp.float32
BF16 = jnp.bfloat16
DP = ("x", "z")
TENSOR = ("y", "core")
ROUND = ("z", "x")
VMEM_BYTES = 32 * 2**20
VMEM_MOST = 53 * 2**20
STEP = 8


def swap_blocks(blocks, axis):
    return lax.all_to_all(blocks, axis, 0, 0, tiled=True)


def dot(a, b):
    return jnp.dot(a, b, preferred_element_type=F32)


def dot_rows(a, b):
    return lax.dot_general(a, b, (((0,), (0,)), ((), ())), preferred_element_type=F32)


def dot_cols(a, b):
    return lax.dot_general(a, b, (((1,), (1,)), ((), ())), preferred_element_type=F32)


def round_up(count, multiple):
    return -(-count // multiple) * multiple


def two_terms(value):
    high = value.astype(BF16)
    rest = (value - high.astype(F32)).astype(BF16)
    return high, rest


def three_terms(value):
    high = value.astype(BF16)
    rest = value - high.astype(F32)
    middle = rest.astype(BF16)
    low = (rest - middle.astype(F32)).astype(BF16)
    return high.astype(F32), middle.astype(F32), low.astype(F32)


def call(kernel, out_shapes, scratch, flops, bytes_accessed, in_specs, vmem=VMEM_BYTES):
    return pl.pallas_call(
        kernel,
        out_shape=out_shapes,
        in_specs=in_specs,
        scratch_shapes=scratch,
        compiler_params=pltpu.CompilerParams(vmem_limit_bytes=vmem),
        cost_estimate=pl.CostEstimate(flops=flops, bytes_accessed=bytes_accessed, transcendentals=0),
    )


IN_VMEM = pl.BlockSpec(memory_space=pltpu.VMEM)
ANYWHERE = pl.BlockSpec(memory_space=pl.ANY)


def fetch(sources, targets, sems):
    copies = []
    for index, (source, target) in enumerate(zip(sources, targets)):
        copies.append(pltpu.make_async_copy(source, target, sems.at[index]))
        copies[-1].start()
    return copies


def token_term_kernel(hid_hbm, out_hbm, q_hbm, o_ref, own_ref, hid, out, q, sems):
    rank = q.shape[1]
    half = own_ref.shape[0]
    copies = fetch([q_hbm, out_hbm, hid_hbm], [q, out, hid], sems)
    side = lax.axis_index("z") % 2
    copies[0].wait()
    own_ref[...] = q[pl.ds(pl.multiple_of(side * half, 128), half), :]
    copies[1].wait()
    high, rest = two_terms(dot(out[...], q[...]))
    both = jnp.concatenate([high, rest], axis=1)
    copies[2].wait()
    turned = dot_rows(hid[...], both)
    o_ref[...] = turned[:, :rank] + turned[:, rank:]


def token_term(hidden, grad_out, q_whole, half):
    tokens, rows = hidden.shape
    width, rank = q_whole.shape
    return call(
        token_term_kernel,
        (
            jax.ShapeDtypeStruct((rows, rank), F32),
            jax.ShapeDtypeStruct((half, rank), BF16),
        ),
        [
            pltpu.VMEM((tokens, rows), BF16),
            pltpu.VMEM((tokens, width), BF16),
            pltpu.VMEM((width, rank), BF16),
            pltpu.SemaphoreType.DMA((3,)),
        ],
        2 * rank * tokens * (width + 2 * rows),
        2 * (tokens * (width + rows) + width * rank),
        [ANYWHERE] * 3,
        VMEM_MOST,
    )(hidden, grad_out, q_whole)


def left_term_kernel(err_ref, own_ref, token_ref, o_ref):
    rows, rank = token_ref.shape
    term = dot(err_ref[0], own_ref[...]) + token_ref[...]
    blocks, chunk, _ = o_ref.shape
    for i in range(blocks):
        piece = term[min(i * chunk, rows) : min((i + 1) * chunk, rows)]
        missing = chunk - piece.shape[0]
        if missing == chunk:
            piece = jnp.zeros((chunk, rank), F32)
        elif missing:
            piece = jnp.concatenate([piece, jnp.zeros((missing, rank), F32)], axis=0)
        o_ref[i] = piece.astype(BF16)


def left_term(error, q_own, tokens, blocks, chunk):
    rows, rank = tokens.shape
    half = error.shape[2]
    return call(
        left_term_kernel,
        jax.ShapeDtypeStruct((blocks, chunk, rank), BF16),
        [],
        2 * rank * rows * half,
        2 * (rows * half + half * rank),
        [IN_VMEM] * 3,
    )(error, q_own, tokens)


def mean_kernel(scale, in_ref, o_ref):
    blocks = in_ref.shape[0]
    total = in_ref[0].astype(F32)
    for i in range(1, blocks):
        total += in_ref[i].astype(F32)
    total = (total * scale).astype(BF16)
    for i in range(blocks):
        o_ref[i] = total


def mean_of_blocks(blocks, scale):
    return call(
        functools.partial(mean_kernel, scale),
        jax.ShapeDtypeStruct(blocks.shape, BF16),
        [],
        blocks.size,
        4 * blocks.size,
        [IN_VMEM],
    )(blocks)


def right_term_kernel(n_x, n_tensor, hid_ref, out_ref, err_ref, p_ref, send_ref, keep_ref, turned, flat, gram):
    rows = hid_ref.shape[1]
    width = out_ref.shape[1]
    half = err_ref.shape[2]
    rank = p_ref.shape[1]
    x, z, core = (lax.axis_index(axis) for axis in ("x", "z", "core"))
    quarter = rows // n_x
    p_quarter = p_ref[pl.ds(pl.multiple_of(x * quarter, 16), quarter), :]
    gram[...] = dot_rows(p_quarter, p_quarter)
    p_own = p_ref[:rows, :]
    high, rest = two_terms(dot(hid_ref[...], p_own))
    both = jnp.concatenate([high, rest], axis=1)
    from_err = dot_rows(p_own, err_ref[0])
    from_out = dot_rows(both, out_ref[...])
    turned[...] = from_out[:rank] + from_out[rank:]
    side = z % 2
    mine = pl.ds(pl.multiple_of(side * half, 128), half)
    turned[:, mine] += from_err
    for i in range(width // rank):
        flat[i * rank : (i + 1) * rank, :] = jnp.transpose(turned[:, i * rank : (i + 1) * rank])
    block = width // n_tensor
    blocks = n_tensor // 2
    for target, owner in ((send_ref, 1 - core), (keep_ref, core)):
        for i in range(blocks):
            start = pl.multiple_of((2 * i + owner) * block, 8)
            target[i * block : (i + 1) * block, :] = flat[pl.ds(start, block), :]
        few = target.shape[0] - blocks * block
        target[blocks * block :, :] = gram[pl.ds(pl.multiple_of(z * few, 8), few), :]


def right_terms(hidden, grad_out, error, p_sum, n_x, n_z, n_tensor):
    tokens, rows = hidden.shape
    width = grad_out.shape[1]
    half = error.shape[2]
    rank = p_sum.shape[1]
    kept = jax.ShapeDtypeStruct((width // 2 + rank // n_z, rank), F32)
    return call(
        functools.partial(right_term_kernel, n_x, n_tensor),
        (kept, kept),
        [
            pltpu.VMEM((rank, width), F32),
            pltpu.VMEM((width, rank), F32),
            pltpu.VMEM((rank, rank), F32),
        ],
        2 * rank * (tokens * (width + rows) + rows * half),
        2 * (tokens * (width + rows) + rows * half + rows * rank),
        [IN_VMEM] * 4,
    )(hidden, grad_out, error, p_sum)


def pack_kernel(n_x, piece, few, keep_ref, came_ref, o_ref, total, pack):
    total[...] = keep_ref[...] + came_ref[...]
    count = o_ref.shape[0]
    terms = three_terms(total[count * piece :, :])
    for i in range(count):
        at = i % n_x
        pack[i, 0:piece, :] = total[i * piece : (i + 1) * piece, :]
        for j, term in enumerate(terms):
            pack[i, piece + j * few : piece + (j + 1) * few, :] = term[at * few : (at + 1) * few]
    o_ref[...] = pack[...].astype(BF16)


def packets_of(kept, came, n_x, count, few):
    rows, rank = kept.shape
    piece = (rows - n_x * few) // count
    deep = piece + 3 * few
    return call(
        functools.partial(pack_kernel, n_x, piece, few),
        jax.ShapeDtypeStruct((count, deep, rank), BF16),
        [pltpu.VMEM((rows, rank), F32), pltpu.VMEM((count, deep, rank), F32)],
        rows * rank,
        8 * rows * rank + 2 * count * deep * rank,
        [IN_VMEM, IN_VMEM],
    )(kept, came)


def repack_kernel(few, in_ref, o_ref, pack):
    count, deep, rank = in_ref.shape
    piece = deep - 3 * few
    total = in_ref[0].astype(F32)
    for i in range(1, count):
        total += in_ref[i].astype(F32)
    pack[...] = total
    rows = [pack[piece + j * few : piece + (j + 1) * few, :] for j in range(3)]
    for j, term in enumerate(three_terms((rows[2] + rows[1]) + rows[0])):
        pack[piece + j * few : piece + (j + 1) * few, :] = term
    packet = pack[...].astype(BF16)
    for i in range(o_ref.shape[0]):
        o_ref[i] = packet


def repacked(packets, few, n_dp):
    count, deep, rank = packets.shape
    return call(
        functools.partial(repack_kernel, few),
        jax.ShapeDtypeStruct((n_dp, deep, rank), BF16),
        [pltpu.VMEM((deep, rank), F32)],
        packets.size,
        4 * packets.size,
        [IN_VMEM],
    )(packets)


def small_factor(block, like):
    size = block.shape[0]
    a = {}
    for i in range(size):
        for j in range(i + 1):
            a[i, j] = jnp.broadcast_to(block[i : i + 1, j : j + 1], like)
    inverse = {}
    for j in range(size):
        scale = lax.rsqrt(a[j, j])
        for m in range(j):
            inverse[j, m] = inverse[j, m] * scale
        inverse[j, j] = scale
        column = {i: a[i, j] * scale for i in range(j + 1, size)}
        for i in range(j + 1, size):
            for m in range(j + 1, i + 1):
                a[i, m] = a[i, m] - column[i] * column[m]
            for m in range(j + 1):
                step = column[i] * inverse[j, m]
                inverse[i, m] = inverse[i, m] - step if (i, m) in inverse else -step
    return inverse


def inverse_factor(gram):
    rank = gram.shape[0]
    like = (STEP, rank)
    lane = lax.broadcasted_iota(jnp.int32, like, 1)
    tiles = [gram[b * STEP : (b + 1) * STEP, :] for b in range(rank // STEP)]
    done = []
    for k in range(rank // STEP):
        first = k * STEP
        inverse = small_factor(tiles[k][:, first : first + STEP], like)
        inside = (lane >= first) & (lane < first + STEP)
        pivots = []
        for m in range(STEP):
            row = jnp.broadcast_to(tiles[k][m : m + 1, :], like)
            pivots.append(jnp.where(inside, jnp.where(lane == first + m, 1.0, 0.0), row))
        scaled = []
        for i in range(STEP):
            row = inverse[i, 0] * pivots[0]
            for m in range(1, i + 1):
                row = row + inverse[i, m] * pivots[m]
            scaled.append(row)
        sublane = lax.broadcasted_iota(jnp.int32, like, 0)
        rows = scaled[0]
        for i in range(1, STEP):
            rows = jnp.where(sublane == i, scaled[i], rows)
        done.append(jnp.where(lane <= first + sublane, rows, 0.0))
        for b in range(k + 1, rank // STEP):
            columns = [
                jnp.broadcast_to(tiles[b][:, first + m : first + m + 1], like) for m in range(STEP)
            ]
            tile = jnp.where(inside, 0.0, tiles[b])
            for i in range(STEP):
                factor = inverse[i, 0] * columns[0]
                for m in range(1, i + 1):
                    factor = factor + inverse[i, m] * columns[m]
                tile = tile - factor * scaled[i]
            tiles[b] = tile
    return jnp.concatenate(done, axis=0)


def finish_kernel(scale, pick_ref, in_ref, p_ref, p_out, q_out):
    rank = p_ref.shape[1]
    inverse = inverse_factor(dot(pick_ref[:rank, :], in_ref[...]))
    s_sum = dot(pick_ref[rank:, :], in_ref[...]) * scale
    terms = [term.astype(BF16) for term in three_terms(inverse)]
    p_low = p_ref[: p_out.shape[0], :]
    p_new = dot_cols(p_low, terms[2]) + dot_cols(p_low, terms[1])
    p_out[...] = (p_new + dot_cols(p_low, terms[0])).astype(BF16)
    q_new = lax.dot_general(
        s_sum,
        inverse,
        (((1,), (1,)), ((), ())),
        precision=lax.Precision.HIGHEST,
        preferred_element_type=F32,
    )
    q_out[...] = q_new.astype(BF16)


def pick_rows(n_x, n_z, piece, few, rank):
    deep = piece + 3 * few
    source = np.arange(n_x * n_z * deep)
    device, row = source // deep, source % deep
    z, x = device // n_x, device % n_x
    gram_row = (z * n_x + x) * few + (row - piece) % few
    target = np.where(row < piece, rank + x * piece + row, gram_row)
    return (np.arange(rank + n_x * piece)[:, None] == target[None, :]).astype(ml_dtypes.bfloat16)


def finished(pick, packets, p_sum, rows, n_x, few):
    count, deep, rank = packets.shape
    piece = deep - 3 * few
    return call(
        functools.partial(finish_kernel, 2.0 / count),
        (
            jax.ShapeDtypeStruct((rows, rank), BF16),
            jax.ShapeDtypeStruct((n_x * piece, rank), BF16),
        ),
        [],
        2 * rank * (pick.size + 3 * rows * rank),
        2 * (pick.size + 2 * rows * rank),
        [IN_VMEM, IN_VMEM, IN_VMEM],
    )(pick, packets.reshape(count * deep, rank), p_sum)


def shards(hidden, grad_out, q_init, error):
    n_x, n_z = lax.axis_size("x"), lax.axis_size("z")
    n_dp, n_tensor = lax.axis_size(DP), lax.axis_size(TENSOR)
    replicas = n_dp // 2
    rows, rank = hidden.shape[1], q_init.shape[1]
    few = rank // n_dp
    chunk = round_up(-(-rows // n_dp), 8)

    q_whole = lax.all_gather(q_init, TENSOR, axis=0, tiled=True)
    tokens, q_own = token_term(hidden, grad_out, q_whole, error.shape[2])
    pieces = left_term(error, q_own, tokens, n_dp, chunk)
    pieces = mean_of_blocks(swap_blocks(pieces, ROUND), 1.0 / replicas)
    p_sum = swap_blocks(pieces, ROUND).reshape(n_dp * chunk, rank)
    sent, kept = right_terms(hidden, grad_out, error, p_sum, n_x, n_z, n_tensor)
    came = lax.ppermute(sent, "core", [(0, 1), (1, 0)])
    packets = packets_of(kept, came, n_x, n_x * (n_tensor // 2), few)
    packets = repacked(swap_blocks(packets, ("y", "x")), few, n_dp)
    pick = pick_rows(n_x, n_z, packets.shape[1] - 3 * few, few, rank)
    return finished(jnp.asarray(pick), swap_blocks(packets, ROUND), p_sum, rows, n_x, few)


def solution(mesh):
    fine = Mesh(mesh.devices.reshape(4, 8, 8, 2), DP + TENSOR)
    in_specs = (P(DP, TENSOR), P(DP, None), P(TENSOR, None), P(DP, TENSOR, None))
    out_specs = (P(TENSOR, None), P(TENSOR, None))
    return jax.shard_map(shards, mesh=fine, in_specs=in_specs, out_specs=out_specs, check_vma=False)
```

```python
import functools

import jax
import jax.numpy as jnp
import ml_dtypes
import numpy as np
from jax import lax
from jax.experimental import pallas as pl
from jax.experimental.pallas import tpu as pltpu
from jax.sharding import Mesh
from jax.sharding import PartitionSpec as P

F32 = jnp.float32
BF16 = jnp.bfloat16
DP = ("x", "z")
TENSOR = ("y", "core")
ROUND = ("z", "x")
VMEM_BYTES = 32 * 2**20
VMEM_MOST = 53 * 2**20
STEP = 8


def swap_blocks(blocks, axis):
    return lax.all_to_all(blocks, axis, 0, 0, tiled=True)


def dot(a, b):
    return jnp.dot(a, b, preferred_element_type=F32)


def dot_rows(a, b):
    return lax.dot_general(a, b, (((0,), (0,)), ((), ())), preferred_element_type=F32)


def dot_cols(a, b):
    return lax.dot_general(a, b, (((1,), (1,)), ((), ())), preferred_element_type=F32)


def round_up(count, multiple):
    return -(-count // multiple) * multiple


def two_terms(value):
    high = value.astype(BF16)
    rest = (value - high.astype(F32)).astype(BF16)
    return high, rest


def three_terms(value):
    high = value.astype(BF16)
    rest = value - high.astype(F32)
    middle = rest.astype(BF16)
    low = (rest - middle.astype(F32)).astype(BF16)
    return high.astype(F32), middle.astype(F32), low.astype(F32)


def call(kernel, out_shapes, scratch, flops, bytes_accessed, in_specs, vmem=VMEM_BYTES):
    return pl.pallas_call(
        kernel,
        out_shape=out_shapes,
        in_specs=in_specs,
        scratch_shapes=scratch,
        compiler_params=pltpu.CompilerParams(vmem_limit_bytes=vmem),
        cost_estimate=pl.CostEstimate(flops=flops, bytes_accessed=bytes_accessed, transcendentals=0),
    )


IN_VMEM = pl.BlockSpec(memory_space=pltpu.VMEM)
ANYWHERE = pl.BlockSpec(memory_space=pl.ANY)


def fetch(sources, targets, sems):
    copies = []
    for index, (source, target) in enumerate(zip(sources, targets)):
        copies.append(pltpu.make_async_copy(source, target, sems.at[index]))
        copies[-1].start()
    return copies


def token_term_kernel(hid_hbm, out_hbm, q_hbm, o_ref, own_ref, hid, out, q, sems):
    rank = q.shape[1]
    half = own_ref.shape[0]
    copies = fetch([q_hbm, out_hbm, hid_hbm], [q, out, hid], sems)
    side = lax.axis_index("z") % 2
    copies[0].wait()
    own_ref[...] = q[pl.ds(pl.multiple_of(side * half, 128), half), :]
    copies[1].wait()
    high, rest = two_terms(dot(out[...], q[...]))
    both = jnp.concatenate([high, rest], axis=1)
    copies[2].wait()
    turned = dot_rows(hid[...], both)
    o_ref[...] = turned[:, :rank] + turned[:, rank:]


def token_term(hidden, grad_out, q_whole, half):
    tokens, rows = hidden.shape
    width, rank = q_whole.shape
    return call(
        token_term_kernel,
        (
            jax.ShapeDtypeStruct((rows, rank), F32),
            jax.ShapeDtypeStruct((half, rank), BF16),
        ),
        [
            pltpu.VMEM((tokens, rows), BF16),
            pltpu.VMEM((tokens, width), BF16),
            pltpu.VMEM((width, rank), BF16),
            pltpu.SemaphoreType.DMA((3,)),
        ],
        2 * rank * tokens * (width + 2 * rows),
        2 * (tokens * (width + rows) + width * rank),
        [ANYWHERE] * 3,
        VMEM_MOST,
    )(hidden, grad_out, q_whole)


def left_term_kernel(err_ref, own_ref, token_ref, o_ref):
    rows, rank = token_ref.shape
    term = dot(err_ref[0], own_ref[...]) + token_ref[...]
    blocks, chunk, _ = o_ref.shape
    for i in range(blocks):
        piece = term[min(i * chunk, rows) : min((i + 1) * chunk, rows)]
        missing = chunk - piece.shape[0]
        if missing == chunk:
            piece = jnp.zeros((chunk, rank), F32)
        elif missing:
            piece = jnp.concatenate([piece, jnp.zeros((missing, rank), F32)], axis=0)
        o_ref[i] = piece.astype(BF16)


def left_term(error, q_own, tokens, blocks, chunk):
    rows, rank = tokens.shape
    half = error.shape[2]
    return call(
        left_term_kernel,
        jax.ShapeDtypeStruct((blocks, chunk, rank), BF16),
        [],
        2 * rank * rows * half,
        2 * (rows * half + half * rank),
        [IN_VMEM] * 3,
    )(error, q_own, tokens)


def mean_kernel(scale, in_ref, o_ref):
    blocks = in_ref.shape[0]
    total = in_ref[0].astype(F32)
    for i in range(1, blocks):
        total += in_ref[i].astype(F32)
    total = (total * scale).astype(BF16)
    for i in range(blocks):
        o_ref[i] = total


def mean_of_blocks(blocks, scale):
    return call(
        functools.partial(mean_kernel, scale),
        jax.ShapeDtypeStruct(blocks.shape, BF16),
        [],
        blocks.size,
        4 * blocks.size,
        [IN_VMEM],
    )(blocks)


def right_term_kernel(n_x, n_tensor, hid_ref, out_ref, err_ref, p_ref, send_ref, keep_ref, turned, flat, gram):
    rows = hid_ref.shape[1]
    width = out_ref.shape[1]
    half = err_ref.shape[2]
    rank = p_ref.shape[1]
    x, z, core = (lax.axis_index(axis) for axis in ("x", "z", "core"))
    quarter = rows // n_x
    p_quarter = p_ref[pl.ds(pl.multiple_of(x * quarter, 16), quarter), :]
    gram[...] = dot_rows(p_quarter, p_quarter)
    p_own = p_ref[:rows, :]
    high, rest = two_terms(dot(hid_ref[...], p_own))
    both = jnp.concatenate([high, rest], axis=1)
    from_err = dot_rows(p_own, err_ref[0])
    from_out = dot_rows(both, out_ref[...])
    turned[...] = from_out[:rank] + from_out[rank:]
    side = z % 2
    mine = pl.ds(pl.multiple_of(side * half, 128), half)
    turned[:, mine] += from_err
    for i in range(width // rank):
        flat[i * rank : (i + 1) * rank, :] = jnp.transpose(turned[:, i * rank : (i + 1) * rank])
    block = width // n_tensor
    blocks = n_tensor // 2
    for target, owner in ((send_ref, 1 - core), (keep_ref, core)):
        for i in range(blocks):
            start = pl.multiple_of((2 * i + owner) * block, 8)
            target[i * block : (i + 1) * block, :] = flat[pl.ds(start, block), :]
        few = target.shape[0] - blocks * block
        target[blocks * block :, :] = gram[pl.ds(pl.multiple_of(z * few, 8), few), :]


def right_terms(hidden, grad_out, error, p_sum, n_x, n_z, n_tensor):
    tokens, rows = hidden.shape
    width = grad_out.shape[1]
    half = error.shape[2]
    rank = p_sum.shape[1]
    kept = jax.ShapeDtypeStruct((width // 2 + rank // n_z, rank), F32)
    return call(
        functools.partial(right_term_kernel, n_x, n_tensor),
        (kept, kept),
        [
            pltpu.VMEM((rank, width), F32),
            pltpu.VMEM((width, rank), F32),
            pltpu.VMEM((rank, rank), F32),
        ],
        2 * rank * (tokens * (width + rows) + rows * half),
        2 * (tokens * (width + rows) + rows * half + rows * rank),
        [IN_VMEM] * 4,
    )(hidden, grad_out, error, p_sum)


def pack_kernel(n_x, piece, few, keep_ref, came_ref, o_ref, total, pack):
    total[...] = keep_ref[...] + came_ref[...]
    count = o_ref.shape[0]
    terms = three_terms(total[count * piece :, :])
    for i in range(count):
        at = i % n_x
        pack[i, 0:piece, :] = total[i * piece : (i + 1) * piece, :]
        for j, term in enumerate(terms):
            pack[i, piece + j * few : piece + (j + 1) * few, :] = term[at * few : (at + 1) * few]
    o_ref[...] = pack[...].astype(BF16)


def packets_of(kept, came, n_x, count, few):
    rows, rank = kept.shape
    piece = (rows - n_x * few) // count
    deep = piece + 3 * few
    return call(
        functools.partial(pack_kernel, n_x, piece, few),
        jax.ShapeDtypeStruct((count, deep, rank), BF16),
        [pltpu.VMEM((rows, rank), F32), pltpu.VMEM((count, deep, rank), F32)],
        rows * rank,
        8 * rows * rank + 2 * count * deep * rank,
        [IN_VMEM, IN_VMEM],
    )(kept, came)


def repack_kernel(few, in_ref, o_ref, pack):
    count, deep, rank = in_ref.shape
    piece = deep - 3 * few
    total = in_ref[0].astype(F32)
    for i in range(1, count):
        total += in_ref[i].astype(F32)
    pack[...] = total
    rows = [pack[piece + j * few : piece + (j + 1) * few, :] for j in range(3)]
    for j, term in enumerate(three_terms((rows[2] + rows[1]) + rows[0])):
        pack[piece + j * few : piece + (j + 1) * few, :] = term
    packet = pack[...].astype(BF16)
    for i in range(o_ref.shape[0]):
        o_ref[i] = packet


def repacked(packets, few, n_dp):
    count, deep, rank = packets.shape
    return call(
        functools.partial(repack_kernel, few),
        jax.ShapeDtypeStruct((n_dp, deep, rank), BF16),
        [pltpu.VMEM((deep, rank), F32)],
        packets.size,
        4 * packets.size,
        [IN_VMEM],
    )(packets)


def across(tile, column):
    return jnp.broadcast_to(tile[:, column : column + 1], tile.shape)


def down(tile, row):
    return jnp.broadcast_to(tile[row : row + 1, :], tile.shape)


def small_factor(columns):
    size = len(columns)
    a = {(i, j): down(columns[j], i) for i in range(size) for j in range(i + 1)}
    inverse = {}
    for j in range(size):
        scale = lax.rsqrt(a[j, j])
        for m in range(j):
            inverse[j, m] = inverse[j, m] * scale
        inverse[j, j] = scale
        column = {i: a[i, j] * scale for i in range(j + 1, size)}
        for i in range(j + 1, size):
            for m in range(j + 1, i + 1):
                a[i, m] = a[i, m] - column[i] * column[m]
            for m in range(j + 1):
                step = column[i] * inverse[j, m]
                inverse[i, m] = inverse[i, m] - step if (i, m) in inverse else -step
    return inverse


def weighted(inverse, items, row):
    total = inverse[row, 0] * items[0]
    for m in range(1, row + 1):
        total = total + inverse[row, m] * items[m]
    return total


def inverse_factor(gram):
    rank = gram.shape[0]
    count = rank // STEP
    lane = lax.broadcasted_iota(jnp.int32, (STEP, rank), 1)
    sublane = lax.broadcasted_iota(jnp.int32, (STEP, rank), 0)
    tiles = [gram[b * STEP : (b + 1) * STEP, :] for b in range(count)]
    block = [across(tiles[0], j) for j in range(STEP)]
    done = []
    for k in range(count):
        first = k * STEP
        inverse = small_factor(block)
        inside = (lane >= first) & (lane < first + STEP)
        pivots = []
        for m in range(STEP):
            unit = jnp.where(lane == first + m, 1.0, 0.0)
            pivots.append(jnp.where(inside, unit, down(tiles[k], m)))
        scaled = [weighted(inverse, pivots, i) for i in range(STEP)]
        rows = scaled[0]
        for i in range(1, STEP):
            rows = jnp.where(sublane == i, scaled[i], rows)
        done.append(jnp.where(lane <= first + sublane, rows, 0.0))
        solved = []
        for m in range(STEP):
            row = inverse[m, m] * scaled[m]
            for i in range(m + 1, STEP):
                row = row + inverse[i, m] * scaled[i]
            solved.append(row)
        for b in range(k + 1, count):
            columns = [across(tiles[b], first + m) for m in range(STEP)]
            tile = jnp.where(inside, 0.0, tiles[b])
            if b == k + 1:
                block = [across(tiles[b], first + STEP + j) for j in range(STEP)]
                factors = [weighted(inverse, columns, i) for i in range(STEP)]
                for i, factor in enumerate(factors):
                    tile = tile - factor * scaled[i]
                    block = [block[j] - factor * down(factor, j) for j in range(STEP)]
            else:
                for m in range(STEP):
                    tile = tile - columns[m] * solved[m]
            tiles[b] = tile
    return jnp.concatenate(done, axis=0)


def finish_kernel(scale, pick_ref, in_ref, p_ref, p_out, q_out):
    rank = p_ref.shape[1]
    inverse = inverse_factor(dot(pick_ref[:rank, :], in_ref[...]))
    s_sum = dot(pick_ref[rank:, :], in_ref[...]) * scale
    terms = [term.astype(BF16) for term in three_terms(inverse)]
    p_low = p_ref[: p_out.shape[0], :]
    p_new = dot_cols(p_low, terms[2]) + dot_cols(p_low, terms[1])
    p_out[...] = (p_new + dot_cols(p_low, terms[0])).astype(BF16)
    q_new = lax.dot_general(
        s_sum,
        inverse,
        (((1,), (1,)), ((), ())),
        precision=lax.Precision.HIGHEST,
        preferred_element_type=F32,
    )
    q_out[...] = q_new.astype(BF16)


def pick_rows(n_x, n_z, piece, few, rank):
    deep = piece + 3 * few
    source = np.arange(n_x * n_z * deep)
    device, row = source // deep, source % deep
    z, x = device // n_x, device % n_x
    gram_row = (z * n_x + x) * few + (row - piece) % few
    target = np.where(row < piece, rank + x * piece + row, gram_row)
    return (np.arange(rank + n_x * piece)[:, None] == target[None, :]).astype(ml_dtypes.bfloat16)


def finished(pick, packets, p_sum, rows, n_x, few):
    count, deep, rank = packets.shape
    piece = deep - 3 * few
    return call(
        functools.partial(finish_kernel, 2.0 / count),
        (
            jax.ShapeDtypeStruct((rows, rank), BF16),
            jax.ShapeDtypeStruct((n_x * piece, rank), BF16),
        ),
        [],
        2 * rank * (pick.size + 3 * rows * rank),
        2 * (pick.size + 2 * rows * rank),
        [IN_VMEM, IN_VMEM, IN_VMEM],
    )(pick, packets.reshape(count * deep, rank), p_sum)


def shards(hidden, grad_out, q_init, error):
    n_x, n_z = lax.axis_size("x"), lax.axis_size("z")
    n_dp, n_tensor = lax.axis_size(DP), lax.axis_size(TENSOR)
    replicas = n_dp // 2
    rows, rank = hidden.shape[1], q_init.shape[1]
    few = rank // n_dp
    chunk = round_up(-(-rows // n_dp), 8)

    q_whole = lax.all_gather(q_init, TENSOR, axis=0, tiled=True)
    tokens, q_own = token_term(hidden, grad_out, q_whole, error.shape[2])
    pieces = left_term(error, q_own, tokens, n_dp, chunk)
    pieces = mean_of_blocks(swap_blocks(pieces, ROUND), 1.0 / replicas)
    p_sum = swap_blocks(pieces, ROUND).reshape(n_dp * chunk, rank)
    sent, kept = right_terms(hidden, grad_out, error, p_sum, n_x, n_z, n_tensor)
    came = lax.ppermute(sent, "core", [(0, 1), (1, 0)])
    packets = packets_of(kept, came, n_x, n_x * (n_tensor // 2), few)
    packets = repacked(swap_blocks(packets, ("y", "x")), few, n_dp)
    pick = pick_rows(n_x, n_z, packets.shape[1] - 3 * few, few, rank)
    return finished(jnp.asarray(pick), swap_blocks(packets, ROUND), p_sum, rows, n_x, few)


def solution(mesh):
    fine = Mesh(mesh.devices.reshape(4, 8, 8, 2), DP + TENSOR)
    in_specs = (P(DP, TENSOR), P(DP, None), P(TENSOR, None), P(DP, TENSOR, None))
    out_specs = (P(TENSOR, None), P(TENSOR, None))
    return jax.shard_map(shards, mesh=fine, in_specs=in_specs, out_specs=out_specs, check_vma=False)
```

```python
import functools

import jax
import jax.numpy as jnp
import ml_dtypes
import numpy as np
from jax import lax
from jax.experimental import pallas as pl
from jax.experimental.pallas import tpu as pltpu
from jax.sharding import Mesh
from jax.sharding import PartitionSpec as P

F32 = jnp.float32
BF16 = jnp.bfloat16
DP = ("x", "z")
TENSOR = ("y", "core")
ROUND = ("z", "x")
VMEM_BYTES = 32 * 2**20
VMEM_MOST = 51 * 2**20
STEP = 8


def swap_blocks(blocks, axis):
    return lax.all_to_all(blocks, axis, 0, 0, tiled=True)


def dot(a, b):
    return jnp.dot(a, b, preferred_element_type=F32)


def dot_rows(a, b):
    return lax.dot_general(a, b, (((0,), (0,)), ((), ())), preferred_element_type=F32)


def dot_cols(a, b):
    return lax.dot_general(a, b, (((1,), (1,)), ((), ())), preferred_element_type=F32)


def round_up(count, multiple):
    return -(-count // multiple) * multiple


def two_terms(value):
    high = value.astype(BF16)
    rest = (value - high.astype(F32)).astype(BF16)
    return high, rest


def three_terms(value):
    high = value.astype(BF16)
    rest = value - high.astype(F32)
    middle = rest.astype(BF16)
    low = (rest - middle.astype(F32)).astype(BF16)
    return high.astype(F32), middle.astype(F32), low.astype(F32)


def call(kernel, out_shapes, scratch, flops, bytes_accessed, in_specs, vmem=VMEM_BYTES):
    return pl.pallas_call(
        kernel,
        out_shape=out_shapes,
        in_specs=in_specs,
        scratch_shapes=scratch,
        compiler_params=pltpu.CompilerParams(vmem_limit_bytes=vmem),
        cost_estimate=pl.CostEstimate(flops=flops, bytes_accessed=bytes_accessed, transcendentals=0),
    )


IN_VMEM = pl.BlockSpec(memory_space=pltpu.VMEM)
ANYWHERE = pl.BlockSpec(memory_space=pl.ANY)


def fetch(sources, targets, sems):
    copies = []
    for index, (source, target) in enumerate(zip(sources, targets)):
        copies.append(pltpu.make_async_copy(source, target, sems.at[index]))
        copies[-1].start()
    return copies


def token_term_kernel(hid_hbm, out_hbm, q_hbm, o_ref, own_ref, hid, out, q, sems):
    rank = q.shape[1]
    half = own_ref.shape[0]
    copies = fetch([q_hbm, out_hbm, hid_hbm], [q, out, hid], sems)
    side = lax.axis_index("z") % 2
    copies[0].wait()
    own_ref[...] = q[pl.ds(pl.multiple_of(side * half, 128), half), :]
    copies[1].wait()
    high, rest = two_terms(dot(out[...], q[...]))
    both = jnp.concatenate([high, rest], axis=1)
    copies[2].wait()
    turned = dot_rows(hid[...], both)
    o_ref[...] = turned[:, :rank] + turned[:, rank:]


def token_term(hidden, grad_out, q_whole, half):
    tokens, rows = hidden.shape
    width, rank = q_whole.shape
    return call(
        token_term_kernel,
        (
            jax.ShapeDtypeStruct((rows, rank), F32),
            jax.ShapeDtypeStruct((half, rank), BF16),
        ),
        [
            pltpu.VMEM((tokens, rows), BF16),
            pltpu.VMEM((tokens, width), BF16),
            pltpu.VMEM((width, rank), BF16),
            pltpu.SemaphoreType.DMA((3,)),
        ],
        2 * rank * tokens * (width + 2 * rows),
        2 * (tokens * (width + rows) + width * rank),
        [ANYWHERE] * 3,
        VMEM_MOST,
    )(hidden, grad_out, q_whole)


def left_term_kernel(err_ref, own_ref, token_ref, o_ref):
    rows, rank = token_ref.shape
    term = dot(err_ref[0], own_ref[...]) + token_ref[...]
    blocks, chunk, _ = o_ref.shape
    for i in range(blocks):
        piece = term[min(i * chunk, rows) : min((i + 1) * chunk, rows)]
        missing = chunk - piece.shape[0]
        if missing == chunk:
            piece = jnp.zeros((chunk, rank), F32)
        elif missing:
            piece = jnp.concatenate([piece, jnp.zeros((missing, rank), F32)], axis=0)
        o_ref[i] = piece.astype(BF16)


def left_term(error, q_own, tokens, blocks, chunk):
    rows, rank = tokens.shape
    half = error.shape[2]
    return call(
        left_term_kernel,
        jax.ShapeDtypeStruct((blocks, chunk, rank), BF16),
        [],
        2 * rank * rows * half,
        2 * (rows * half + half * rank),
        [IN_VMEM] * 3,
    )(error, q_own, tokens)


def mean_kernel(scale, in_ref, o_ref):
    blocks = in_ref.shape[0]
    total = in_ref[0].astype(F32)
    for i in range(1, blocks):
        total += in_ref[i].astype(F32)
    total = (total * scale).astype(BF16)
    for i in range(blocks):
        o_ref[i] = total


def mean_of_blocks(blocks, scale):
    return call(
        functools.partial(mean_kernel, scale),
        jax.ShapeDtypeStruct(blocks.shape, BF16),
        [],
        blocks.size,
        4 * blocks.size,
        [IN_VMEM],
    )(blocks)


def right_term_kernel(n_x, n_tensor, hid_ref, out_ref, err_ref, p_ref, send_ref, keep_ref, turned, flat, gram):
    rows = hid_ref.shape[1]
    width = out_ref.shape[1]
    half = err_ref.shape[2]
    rank = p_ref.shape[1]
    x, z, core = (lax.axis_index(axis) for axis in ("x", "z", "core"))
    quarter = rows // n_x
    p_quarter = p_ref[pl.ds(pl.multiple_of(x * quarter, 16), quarter), :]
    gram[...] = dot_rows(p_quarter, p_quarter)
    p_own = p_ref[:rows, :]
    high, rest = two_terms(dot(hid_ref[...], p_own))
    both = jnp.concatenate([high, rest], axis=1)
    from_err = dot_rows(p_own, err_ref[0])
    from_out = dot_rows(both, out_ref[...])
    turned[...] = from_out[:rank] + from_out[rank:]
    side = z % 2
    mine = pl.ds(pl.multiple_of(side * half, 128), half)
    turned[:, mine] += from_err
    for i in range(width // rank):
        flat[i * rank : (i + 1) * rank, :] = jnp.transpose(turned[:, i * rank : (i + 1) * rank])
    block = width // n_tensor
    blocks = n_tensor // 2
    for target, owner in ((send_ref, 1 - core), (keep_ref, core)):
        for i in range(blocks):
            start = pl.multiple_of((2 * i + owner) * block, 8)
            target[i * block : (i + 1) * block, :] = flat[pl.ds(start, block), :]
        few = target.shape[0] - blocks * block
        target[blocks * block :, :] = gram[pl.ds(pl.multiple_of(z * few, 8), few), :]


def right_terms(hidden, grad_out, error, p_sum, n_x, n_z, n_tensor):
    tokens, rows = hidden.shape
    width = grad_out.shape[1]
    half = error.shape[2]
    rank = p_sum.shape[1]
    kept = jax.ShapeDtypeStruct((width // 2 + rank // n_z, rank), F32)
    return call(
        functools.partial(right_term_kernel, n_x, n_tensor),
        (kept, kept),
        [
            pltpu.VMEM((rank, width), F32),
            pltpu.VMEM((width, rank), F32),
            pltpu.VMEM((rank, rank), F32),
        ],
        2 * rank * (tokens * (width + rows) + rows * half),
        2 * (tokens * (width + rows) + rows * half + rows * rank),
        [IN_VMEM] * 4,
    )(hidden, grad_out, error, p_sum)


def pack_kernel(n_x, piece, few, keep_ref, came_ref, o_ref, total, pack):
    total[...] = keep_ref[...] + came_ref[...]
    count = o_ref.shape[0]
    terms = three_terms(total[count * piece :, :])
    for i in range(count):
        at = i % n_x
        pack[i, 0:piece, :] = total[i * piece : (i + 1) * piece, :]
        for j, term in enumerate(terms):
            pack[i, piece + j * few : piece + (j + 1) * few, :] = term[at * few : (at + 1) * few]
    o_ref[...] = pack[...].astype(BF16)


def packets_of(kept, came, n_x, count, few):
    rows, rank = kept.shape
    piece = (rows - n_x * few) // count
    deep = piece + 3 * few
    return call(
        functools.partial(pack_kernel, n_x, piece, few),
        jax.ShapeDtypeStruct((count, deep, rank), BF16),
        [pltpu.VMEM((rows, rank), F32), pltpu.VMEM((count, deep, rank), F32)],
        rows * rank,
        8 * rows * rank + 2 * count * deep * rank,
        [IN_VMEM, IN_VMEM],
    )(kept, came)


def repack_kernel(few, in_ref, o_ref, pack):
    count, deep, rank = in_ref.shape
    piece = deep - 3 * few
    total = in_ref[0].astype(F32)
    for i in range(1, count):
        total += in_ref[i].astype(F32)
    pack[...] = total
    rows = [pack[piece + j * few : piece + (j + 1) * few, :] for j in range(3)]
    for j, term in enumerate(three_terms((rows[2] + rows[1]) + rows[0])):
        pack[piece + j * few : piece + (j + 1) * few, :] = term
    packet = pack[...].astype(BF16)
    for i in range(o_ref.shape[0]):
        o_ref[i] = packet


def repacked(packets, few, n_dp):
    count, deep, rank = packets.shape
    return call(
        functools.partial(repack_kernel, few),
        jax.ShapeDtypeStruct((n_dp, deep, rank), BF16),
        [pltpu.VMEM((deep, rank), F32)],
        packets.size,
        4 * packets.size,
        [IN_VMEM],
    )(packets)


def across(tile, column):
    return jnp.broadcast_to(tile[:, column : column + 1], tile.shape)


def down(tile, row):
    return jnp.broadcast_to(tile[row : row + 1, :], tile.shape)


def small_factor(columns):
    size = len(columns)
    a = {(i, j): down(columns[j], i) for i in range(size) for j in range(i + 1)}
    inverse = {}
    for j in range(size):
        scale = lax.rsqrt(a[j, j])
        for m in range(j):
            inverse[j, m] = inverse[j, m] * scale
        inverse[j, j] = scale
        column = {i: a[i, j] * scale for i in range(j + 1, size)}
        for i in range(j + 1, size):
            for m in range(j + 1, i + 1):
                a[i, m] = a[i, m] - column[i] * column[m]
            for m in range(j + 1):
                step = column[i] * inverse[j, m]
                inverse[i, m] = inverse[i, m] - step if (i, m) in inverse else -step
    return inverse


def weighted(inverse, items, row):
    total = inverse[row, 0] * items[0]
    for m in range(1, row + 1):
        total = total + inverse[row, m] * items[m]
    return total


def inverse_factor(gram):
    rank = gram.shape[0]
    count = rank // STEP
    lane = lax.broadcasted_iota(jnp.int32, (STEP, rank), 1)
    sublane = lax.broadcasted_iota(jnp.int32, (STEP, rank), 0)
    tiles = [gram[b * STEP : (b + 1) * STEP, :] for b in range(count)]
    block = [across(tiles[0], j) for j in range(STEP)]
    done = []
    for k in range(count):
        first = k * STEP
        inverse = small_factor(block)
        inside = (lane >= first) & (lane < first + STEP)
        pivots = []
        for m in range(STEP):
            unit = jnp.where(lane == first + m, 1.0, 0.0)
            pivots.append(jnp.where(inside, unit, down(tiles[k], m)))
        scaled = [weighted(inverse, pivots, i) for i in range(STEP)]
        rows = scaled[0]
        for i in range(1, STEP):
            rows = jnp.where(sublane == i, scaled[i], rows)
        done.append(jnp.where(lane <= first + sublane, rows, 0.0))
        solved = []
        for m in range(STEP):
            row = inverse[m, m] * scaled[m]
            for i in range(m + 1, STEP):
                row = row + inverse[i, m] * scaled[i]
            solved.append(row)
        for b in range(k + 1, count):
            columns = [across(tiles[b], first + m) for m in range(STEP)]
            tile = jnp.where(inside, 0.0, tiles[b])
            if b == k + 1:
                block = [across(tiles[b], first + STEP + j) for j in range(STEP)]
                factors = [weighted(inverse, columns, i) for i in range(STEP)]
                for i, factor in enumerate(factors):
                    tile = tile - factor * scaled[i]
                    block = [block[j] - factor * down(factor, j) for j in range(STEP)]
            else:
                for m in range(STEP):
                    tile = tile - columns[m] * solved[m]
            tiles[b] = tile
    return jnp.concatenate(done, axis=0)


def finish_kernel(scale, pick_ref, in_ref, p_ref, p_out, q_out):
    rank = p_ref.shape[1]
    inverse = inverse_factor(dot(pick_ref[:rank, :], in_ref[...]))
    s_sum = dot(pick_ref[rank:, :], in_ref[...]) * scale
    terms = [term.astype(BF16) for term in three_terms(inverse)]
    p_low = p_ref[: p_out.shape[0], :]
    p_new = dot_cols(p_low, terms[2]) + dot_cols(p_low, terms[1])
    p_out[...] = (p_new + dot_cols(p_low, terms[0])).astype(BF16)
    q_new = lax.dot_general(
        s_sum,
        inverse,
        (((1,), (1,)), ((), ())),
        precision=lax.Precision.HIGHEST,
        preferred_element_type=F32,
    )
    q_out[...] = q_new.astype(BF16)


def pick_rows(n_x, n_z, piece, few, rank):
    deep = piece + 3 * few
    source = np.arange(n_x * n_z * deep)
    device, row = source // deep, source % deep
    z, x = device // n_x, device % n_x
    gram_row = (z * n_x + x) * few + (row - piece) % few
    target = np.where(row < piece, rank + x * piece + row, gram_row)
    return (np.arange(rank + n_x * piece)[:, None] == target[None, :]).astype(ml_dtypes.bfloat16)


def finished(pick, packets, p_sum, rows, n_x, few):
    count, deep, rank = packets.shape
    piece = deep - 3 * few
    return call(
        functools.partial(finish_kernel, 2.0 / count),
        (
            jax.ShapeDtypeStruct((rows, rank), BF16),
            jax.ShapeDtypeStruct((n_x * piece, rank), BF16),
        ),
        [],
        2 * rank * (pick.size + 3 * rows * rank),
        2 * (pick.size + 2 * rows * rank),
        [IN_VMEM, IN_VMEM, IN_VMEM],
    )(pick, packets.reshape(count * deep, rank), p_sum)


def shards(hidden, grad_out, q_init, error):
    n_x, n_z = lax.axis_size("x"), lax.axis_size("z")
    n_dp, n_tensor = lax.axis_size(DP), lax.axis_size(TENSOR)
    replicas = n_dp // 2
    rows, rank = hidden.shape[1], q_init.shape[1]
    few = rank // n_dp
    chunk = round_up(-(-rows // n_dp), 8)

    q_whole = lax.all_gather(q_init, TENSOR, axis=0, tiled=True)
    tokens, q_own = token_term(hidden, grad_out, q_whole, error.shape[2])
    pieces = left_term(error, q_own, tokens, n_dp, chunk)
    pieces = mean_of_blocks(swap_blocks(pieces, ROUND), 1.0 / replicas)
    p_sum = swap_blocks(pieces, ROUND).reshape(n_dp * chunk, rank)
    sent, kept = right_terms(hidden, grad_out, error, p_sum, n_x, n_z, n_tensor)
    came = lax.ppermute(sent, "core", [(0, 1), (1, 0)])
    packets = packets_of(kept, came, n_x, n_x * (n_tensor // 2), few)
    packets = repacked(swap_blocks(packets, ("y", "x")), few, n_dp)
    pick = pick_rows(n_x, n_z, packets.shape[1] - 3 * few, few, rank)
    return finished(jnp.asarray(pick), swap_blocks(packets, ROUND), p_sum, rows, n_x, few)


def solution(mesh):
    fine = Mesh(mesh.devices.reshape(4, 8, 8, 2), DP + TENSOR)
    in_specs = (P(DP, TENSOR), P(DP, None), P(TENSOR, None), P(DP, TENSOR, None))
    out_specs = (P(TENSOR, None), P(TENSOR, None))
    return jax.shard_map(shards, mesh=fine, in_specs=in_specs, out_specs=out_specs, check_vma=False)
```
